32 devices in a mesh: parts: 2 (over y), seq: 4 (over z), res: 4 (over x, core).
Axes of the slice: x: 2, y: 2, z: 4, core: 2. Of those that a mesh axis runs over, the one named last changes fastest.
Arguments:
- relatives_stack: bfloat16 [128, 64, 256], P(('parts', 'seq'), 'res'), parts along dimension 0, may hold values from -6 to 6
- edge_embedding: bfloat16 [128, 64, 128], P(('parts', 'res'), 'seq'), parts along dimension 0, may hold values from -6 to 6
- homolog_present: int32 [128, 64], P(('parts', 'seq'), 'res'), parts along dimension 0, may hold values 0 or 1
- amino_present: int32 [128], P(('parts', 'res')), parts along dimension 0, may hold values 0 or 1
- relatives_stretch: float32 [256], replicated, may hold values from 0.1 to 1.9
- joint_qkvg_weights: bfloat16 [256, 1024], replicated, may hold values from -0.375 to 0.375
- edge_to_logit_matrix: float32 [128, 8], replicated, may hold values from -100 to 100
- closing_blend_weights: bfloat16 [256, 256], replicated, may hold values from -2 to 2
- operand_weights: bfloat16 [256, 64], replicated, may hold values from -0.375 to 0.375
- product_to_edge_matrix: bfloat16 [1024, 128], replicated, may hold values from -6 to 6
Outputs:
- attended_stack: bfloat16 [128, 64, 256], P(('parts', 'seq'), 'res'), parts along dimension 0
- pair_output: bfloat16 [128, 64, 128], P(('parts', 'res'), 'seq'), parts along dimension 0
The draws below stay inside these ranges and needn't reach their ends.
There are 2 independent parts, one for each index of `parts`. The reference program is written for one: setup_inputs(seed, part) draws one part's arguments, and reference() takes and returns one part's arrays. A program takes and returns all parts, laid end to end along the dimension named above; an argument that names none is the same for every part. Nothing has to cross between parts.
All inputs are finite; a program needn't handle non-finite values. No bound on the sum of `homolog_present` or of `amino_present` on one device may be relied on, other than what follows from the above.
Results may differ from the reference program's by a relative error of at most 0.019.
The reference program's roundings to bfloat16 on the way count: a program that leaves them out, or rounds other values in their place, can miss the bound.
Values may be sent and summed in bfloat16 or wider, within the bound.
A program may use at most 64 MiB of HBM per device.

```python
import math
import jax
import jax.numpy as jnp
from jax import lax

STACK_DEPTH = 256
PAIR_WIDTH = 128
FOCUS_GROUPS = 8
GROUP_DEPTH = 32
OPERAND_DEPTH = 32
SEQ_DEV = 16
RELATIVES = 64
PROTEIN_LENGTH = 64


def draw_edge_to_logit_matrix(key, part):
    key = jax.random.fold_in(key, 11)
    base = jnp.clip(jax.random.normal(key, (PAIR_WIDTH, FOCUS_GROUPS), jnp.float32), -4.0, 4.0)
    return base / math.sqrt(PAIR_WIDTH)


def touch_ends(array, key, low, top_value):
    place = [jax.random.randint(jax.random.fold_in(key, axis), (), 0, length) for axis, length in enumerate(array.shape)]
    widest = array.shape.index(max(array.shape))
    beside = place[:widest] + [(place[widest] + 1) % array.shape[widest]] + place[widest + 1:]
    return array.at[tuple(place)].set(low).at[tuple(beside)].set(top_value)


def with_spikes(entries, rng, source, target, shards_of, factor):
    owner, partner = [(jnp.arange(entries.shape[position]) // (entries.shape[position] // shards_of)).reshape([-1 if axis == position else 1 for axis in range(entries.ndim)]) for position in (source, target)]
    chosen = jax.random.permutation(rng, shards_of)[partner]
    strong = (owner == chosen) | (owner == (partner + shards_of // 2) % shards_of)
    return jnp.where(strong, factor * entries, entries)


def block_levels(key, extent, pieces, smallest, largest):
    def one(dim, shards_of):
        steps = jax.random.uniform(jax.random.fold_in(jax.random.fold_in(key, 6), dim), (shards_of,), jnp.float32, smallest / len(pieces), largest / len(pieces))
        return jnp.repeat(jnp.exp(steps), extent[dim] // shards_of).reshape((-1,) + (1,) * (len(extent) - dim - 1))

    loudness = one(*pieces[0])
    for cut in pieces[1:]:
        loudness = loudness * one(*cut)
    return loudness


def normal_values(own_key, dims, scale, most, split=(), held_as=jnp.bfloat16):
    factor_of = block_levels(own_key, dims, split, -0.22, 0.18) if split else 1.0
    array = jax.random.normal(own_key, dims, jnp.float32) * scale * factor_of
    return jnp.minimum(jnp.maximum(array, -most), most).astype(held_as)


def heavy_noise(rng, extent, deviation, reach, shards, heavy, held_as=jnp.bfloat16):
    values = deviation * jax.random.normal(rng, extent, jnp.float32)
    if shards:
        values = values * block_levels(rng, extent, shards, -0.22, 0.18)
    return jnp.clip(with_spikes(values, jax.random.fold_in(rng, 3), *heavy), -reach, reach).astype(held_as)


def setup_inputs(seed: int = 0, part: int = 0) -> dict:
    key_of = jax.random.split(jax.random.key(seed), 11)
    part_splits = jax.random.split(jax.random.fold_in(key_of[10], part), 11)
    relatives_stack = heavy_noise(part_splits[0], (RELATIVES, PROTEIN_LENGTH, STACK_DEPTH), 1.0, 6.0, ((0, 4), (1, 4)), (0, 1, 4, 2.0))
    edge_embedding = normal_values(part_splits[1], (PROTEIN_LENGTH, PROTEIN_LENGTH, PAIR_WIDTH), 1.0, 6.0, ((0, 4), (1, 4)))
    homolog_present = touch_ends((jax.random.randint(part_splits[2], (RELATIVES, PROTEIN_LENGTH), 0, 8) < 7).astype(jnp.int32), jax.random.fold_in(part_splits[2], 1), 0, 1)
    amino_present = touch_ends((jax.random.randint(part_splits[3], (PROTEIN_LENGTH,), 0, 4) < 3).astype(jnp.int32), jax.random.fold_in(part_splits[3], 1), 0, 1)
    relatives_stretch = jnp.clip(1.0 + 0.18 * jax.random.normal(key_of[4], (STACK_DEPTH,), jnp.float32), 0.1, 1.9)
    joint_qkvg_weights = normal_values(key_of[5], (STACK_DEPTH, 4 * FOCUS_GROUPS * GROUP_DEPTH), STACK_DEPTH ** -0.5, 0.375)
    edge_to_logit_matrix = draw_edge_to_logit_matrix(jax.random.fold_in(key_of[10], 71), part)
    closing_blend_weights = normal_values(key_of[7], (FOCUS_GROUPS * GROUP_DEPTH, STACK_DEPTH), FOCUS_GROUPS ** -0.5, 2.0)
    operand_weights = normal_values(key_of[8], (STACK_DEPTH, 2 * OPERAND_DEPTH), STACK_DEPTH ** -0.5, 0.375)
    product_to_edge_matrix = normal_values(key_of[9], (OPERAND_DEPTH * OPERAND_DEPTH, PAIR_WIDTH), 1.0, 6.0)
    return {"relatives_stack": relatives_stack, "edge_embedding": edge_embedding, "homolog_present": homolog_present, "amino_present": amino_present, "relatives_stretch": relatives_stretch, "joint_qkvg_weights": joint_qkvg_weights, "edge_to_logit_matrix": edge_to_logit_matrix, "closing_blend_weights": closing_blend_weights, "operand_weights": operand_weights, "product_to_edge_matrix": product_to_edge_matrix}


def standardize_features(values):
    center = lax.optimization_barrier(jnp.mean(values, axis=-1, keepdims=True))
    shifted = values - center
    spread = lax.optimization_barrier(jnp.mean(shifted * shifted, axis=-1, keepdims=True))
    return shifted * lax.rsqrt(spread + 1e-05)

def attend(queries, key_rows, value_rows, usable, bias_block):
    scores = jnp.einsum('nihd,njhd->nhij', queries.astype(jnp.float32), key_rows.astype(jnp.float32))
    scores = scores + jnp.transpose(bias_block.astype(jnp.float32), (2, 0, 1))[None]
    scores = jnp.where(usable[:, None, None, :] > 0, scores, -1000000000.0)
    ceiling = lax.optimization_barrier(jnp.max(scores, axis=-1, keepdims=True))
    raised = jnp.exp(scores - ceiling)
    weights = (raised / lax.optimization_barrier(jnp.sum(raised, axis=-1, keepdims=True))).astype(jnp.bfloat16)
    return jnp.einsum('nhij,njhd->nihd', weights.astype(jnp.float32), value_rows.astype(jnp.float32)).astype(jnp.bfloat16)

def reference(relatives_stack, edge_embedding, homolog_present, amino_present, relatives_stretch, joint_qkvg_weights, edge_to_logit_matrix, closing_blend_weights, operand_weights, product_to_edge_matrix):
    width = FOCUS_GROUPS * GROUP_DEPTH
    valid_entries = (homolog_present * amino_present[None, :]).astype(jnp.float32)
    whitened_stack = (standardize_features(relatives_stack.astype(jnp.float32)) * relatives_stretch).astype(jnp.bfloat16)
    blended_groups = jnp.dot(whitened_stack.reshape(-1, STACK_DEPTH), joint_qkvg_weights, preferred_element_type=jnp.float32)
    blended_groups = blended_groups.reshape(RELATIVES, PROTEIN_LENGTH, 4, FOCUS_GROUPS, GROUP_DEPTH)
    scale = 1.0 / math.sqrt(GROUP_DEPTH)
    queries = (blended_groups[:, :, 0] * scale).astype(jnp.bfloat16)
    key_rows = blended_groups[:, :, 1].astype(jnp.bfloat16)
    value_rows = blended_groups[:, :, 2].astype(jnp.bfloat16)
    gating = jax.nn.sigmoid(blended_groups[:, :, 3])
    pair_normed = standardize_features(edge_embedding.astype(jnp.float32)).reshape(-1, PAIR_WIDTH)
    pair_bias = jnp.dot(pair_normed, edge_to_logit_matrix, precision=lax.Precision.HIGHEST)
    pair_bias = pair_bias.reshape(PROTEIN_LENGTH, PROTEIN_LENGTH, FOCUS_GROUPS).astype(jnp.bfloat16)
    blocks = RELATIVES // SEQ_DEV

    def one_block(parts):
        return attend(parts[0], parts[1], parts[2], parts[3], pair_bias)
    shaped = (SEQ_DEV, PROTEIN_LENGTH, FOCUS_GROUPS, GROUP_DEPTH)
    attended = lax.map(one_block, (queries.reshape((blocks,) + shaped), key_rows.reshape((blocks,) + shaped), value_rows.reshape((blocks,) + shaped), valid_entries.reshape(blocks, SEQ_DEV, PROTEIN_LENGTH)))
    attended = attended.reshape(RELATIVES, PROTEIN_LENGTH, FOCUS_GROUPS, GROUP_DEPTH)
    gated_values = (gating * attended.astype(jnp.float32)).astype(jnp.bfloat16).reshape(-1, width)
    relatives_folded = relatives_stack.astype(jnp.float32).reshape(-1, STACK_DEPTH)
    attended_stack = (relatives_folded + jnp.dot(gated_values, closing_blend_weights, preferred_element_type=jnp.float32)).astype(jnp.bfloat16)
    attended_stack = attended_stack.reshape(RELATIVES, PROTEIN_LENGTH, STACK_DEPTH)
    tensor_averaged = standardize_features(attended_stack.astype(jnp.float32)).astype(jnp.bfloat16)
    operand_couples = jnp.dot(tensor_averaged.reshape(-1, STACK_DEPTH), operand_weights, preferred_element_type=jnp.float32)
    operand_couples = (operand_couples.reshape(RELATIVES, PROTEIN_LENGTH, 2 * OPERAND_DEPTH) * valid_entries[:, :, None]).astype(jnp.bfloat16)
    left = operand_couples[:, :, :OPERAND_DEPTH]
    right = operand_couples[:, :, OPERAND_DEPTH:]
    outer = jnp.einsum('sip,sjq->ijpq', left.astype(jnp.float32), right.astype(jnp.float32))
    outer = outer.reshape(PROTEIN_LENGTH * PROTEIN_LENGTH, OPERAND_DEPTH * OPERAND_DEPTH)
    counts = jnp.dot(valid_entries.T, valid_entries, precision=lax.Precision.HIGHEST)
    update = jnp.dot(outer, product_to_edge_matrix.astype(jnp.float32), precision=lax.Precision.HIGHEST)
    update = update.reshape(PROTEIN_LENGTH, PROTEIN_LENGTH, PAIR_WIDTH)
    pair_output = (edge_embedding.astype(jnp.float32) + update / jnp.maximum(counts, 1.0)[:, :, None]).astype(jnp.bfloat16)
    return (attended_stack, pair_output)
```

```python
import functools
import math

import jax
import jax.numpy as jnp
from jax import lax
from jax.experimental import pallas as pl
from jax.experimental.pallas import tpu as pltpu
from jax.sharding import PartitionSpec as P

MESH = pl.DeviceIdType.MESH
F32 = jnp.float32
BF16 = jnp.bfloat16


def iota(shape, dim):
    return lax.broadcasted_iota(jnp.int32, shape, dim)


def standardize(values):
    center = jnp.mean(values, axis=-1, keepdims=True)
    shifted = values - center
    spread = jnp.mean(shifted * shifted, axis=-1, keepdims=True)
    return shifted * lax.rsqrt(spread + 1e-05)


def dot(a, b, dims=((1,), (0,)), precision=None):
    return lax.dot_general(a, b, (dims, ((), ())), precision=precision, preferred_element_type=F32)


def indicator(condition):
    return jnp.where(condition, 1.0, 0.0).astype(BF16)


def kernel(
    Z,
    R,
    x_hbm,
    edge_ref,
    homolog_ref,
    amino_ref,
    stretch_ref,
    qkvg_hbm,
    logit_ref,
    blend_hbm,
    operand_ref,
    product_hbm,
    y_hbm,
    pair_ref,
    xall,
    qkvg,
    blend,
    product,
    notes,
    usable,
    bias,
    ybuf,
    lbuf,
    rbuf,
    gbuf,
    grouped,
    unfolded,
    local_sem,
    x_send,
    x_recv,
    n_send,
    n_recv,
    y_send,
    y_recv,
    g_send,
    g_recv,
):
    N, I, W = x_hbm.shape
    C, E = edge_ref.shape[1:]
    H = logit_ref.shape[1]
    DH = blend_hbm.shape[0] // H
    Q = operand_ref.shape[1] // 2
    S = N // R
    L = R * I
    D = R * Z
    T = S * L
    G = 128 // Q
    PH = Q // G
    GB = max(1, I * C // 128)
    IG = I // GB

    part = lax.axis_index("parts")
    z = lax.axis_index("seq")
    r = lax.axis_index("res")
    me = r * Z + z

    loads = [
        pltpu.make_async_copy(x_hbm.at[pl.ds(r * S, S)], xall.at[r], local_sem.at[0]),
        pltpu.make_async_copy(qkvg_hbm, qkvg, local_sem.at[1]),
        pltpu.make_async_copy(blend_hbm, blend, local_sem.at[2]),
        pltpu.make_async_copy(product_hbm, product, local_sem.at[3]),
    ]
    for load in loads:
        load.start()

    def peer(k):
        other = lax.rem(me + k, D)
        return other // Z, lax.rem(other, Z)

    barrier = pltpu.get_barrier_semaphore()

    def greet(k, carry):
        pr, pz = peer(k)
        pl.semaphore_signal(barrier, inc=1, device_id=(part, pz, pr), device_id_type=MESH)
        return carry

    lax.fori_loop(1, D, greet, 0)
    pl.semaphore_wait(barrier, D - 1)

    def x_copy(k):
        pr = lax.rem(r + k, R)
        return pltpu.make_async_remote_copy(
            src_ref=x_hbm.at[pl.ds(pr * S, S)],
            dst_ref=xall.at[r],
            send_sem=x_send,
            recv_sem=x_recv,
            device_id=(part, z, pr),
            device_id_type=MESH,
        )

    for k in range(1, R):
        x_copy(k).start()

    edge = edge_ref[...].astype(F32).reshape(I * C, E)
    bias_rows = dot(
        jnp.transpose(logit_ref[...]), standardize(edge), ((1,), (1,)), lax.Precision.HIGHEST
    )
    width = IG * C
    pieces = [bias_rows[:, g * width : (g + 1) * width] for g in range(GB)]
    bias_rows = jnp.concatenate(pieces, axis=0) if GB > 1 else pieces[0]
    bias_rows = jnp.pad(bias_rows, ((0, 16 - GB * H), (0, 128 - width)))
    valid = (homolog_ref[...] * amino_ref[...][None, :]).astype(F32)
    notes[me, :, 0:128] = bias_rows.astype(BF16)
    notes[me, :, 128:256] = jnp.pad(valid, ((0, 0), (0, 128 - I))).astype(BF16)

    def send_notes(k, carry):
        pr, pz = peer(k)
        pltpu.make_async_remote_copy(
            src_ref=notes.at[me],
            dst_ref=notes.at[me],
            send_sem=n_send,
            recv_sem=n_recv,
            device_id=(part, pz, pr),
            device_id_type=MESH,
        ).start()
        return carry

    lax.fori_loop(1, D, send_notes, 0)

    lane = iota((2 * Q, 128), 1)
    channel = iota((2 * Q, 128), 0)
    spread_left = [indicator(channel == lax.rem(lane, PH) * G + g) for g in range(G)]
    spread_right = indicator(channel == Q + lax.rem(lane, Q))
    spread = jnp.concatenate(spread_left + [spread_right], axis=1)
    operand = dot(operand_ref[...], spread).astype(BF16)

    def all_but_one(ref, sem):
        window = ref.at[pl.ds(0, ref.shape[0] - 1)]
        return pltpu.make_async_copy(window, window, sem)

    loads[0].wait()
    loads[1].wait()
    all_but_one(xall, x_recv).wait()
    x = jnp.concatenate(
        [xall[rr, s] for s in range(S) for rr in range(R)], axis=0
    ).astype(F32)
    normed = (standardize(x) * stretch_ref[...][None, :]).astype(BF16)
    HW = H * DH
    queries = (dot(normed, qkvg[:, 0:HW]) * (1.0 / math.sqrt(DH))).astype(BF16)
    keys = dot(normed, qkvg[:, HW : 2 * HW]).astype(BF16)
    values = dot(normed, qkvg[:, 2 * HW : 3 * HW]).astype(BF16)
    gating = jax.nn.sigmoid(dot(normed, qkvg[:, 3 * HW : 4 * HW]))

    head_of_lane = iota((1, HW), 1) // DH
    head_masks = [indicator(head_of_lane == h) for h in range(H)]

    def raw_scores(s):
        q = queries[s * L : (s + 1) * L]
        expanded = jnp.concatenate([q * head_masks[h] for h in range(H)], axis=0)
        return dot(expanded, keys[s * L : (s + 1) * L], ((1,), (1,)))

    all_but_one(notes, n_recv).wait()
    KZ = Z * 128
    row = iota((KZ, L), 0)
    fold = indicator(
        ((row % 128) % C + (row // 128) * C == iota((KZ, L), 1)) & (row % 128 < width)
    )
    own_lane = jnp.where((iota((IG, KZ), 1) % 128) // C == iota((IG, KZ), 0), 1.0, 0.0)
    for rr in range(R):
        wide = jnp.concatenate(
            [notes[rr * Z + zz, :, 0:128] for zz in range(Z)], axis=1
        ).astype(F32)[: GB * H]
        wide = (wide[:, None, :] * own_lane[None]).reshape(GB * H * IG, KZ).astype(BF16)
        block = dot(wide, fold).reshape(GB, H, IG, L)
        for g in range(GB):
            bias[:, pl.ds(rr * I + g * IG, IG), :] = block[g]

    mask_rows = jnp.concatenate([notes[rr * Z + z, :, 128:256] for rr in range(R)], axis=1)
    prow = iota((R * 128, L), 0)
    place = indicator(
        (prow % 128 + (prow // 128) * I == iota((R * 128, L), 1)) & (prow % 128 < I)
    )
    usable[...] = dot(mask_rows, place)
    usable_rows = [usable[pl.ds(r * S + s, 1), :] for s in range(S)]
    pair_bias = bias[...].reshape(H * L, L)

    attended = []
    for s in range(S):
        scores = raw_scores(s) + pair_bias
        scores = jnp.where(usable_rows[s] > 0, scores, -1000000000.0)
        raised = jnp.exp(scores - jnp.max(scores, axis=-1, keepdims=True))
        weights = (raised * (1.0 / jnp.sum(raised, axis=-1, keepdims=True))).astype(BF16)
        mixed = dot(weights, values[s * L : (s + 1) * L])
        total = mixed[0:L] * head_masks[0].astype(F32)
        for h in range(1, H):
            total = total + mixed[h * L : (h + 1) * L] * head_masks[h].astype(F32)
        attended.append(total.astype(BF16))
    attended = jnp.concatenate(attended, axis=0).astype(F32)
    gated = (gating * attended).astype(BF16)
    loads[2].wait()
    stack = (x + dot(gated, blend[...])).astype(BF16)
    for s in range(S):
        for rr in range(R):
            start = s * L + rr * I
            ybuf[rr, s] = stack[start : start + I]

    def y_copy(k):
        pr = lax.rem(r + k, R)
        return pltpu.make_async_remote_copy(
            src_ref=ybuf.at[pr],
            dst_ref=y_hbm.at[pl.ds(r * S, S)],
            send_sem=y_send,
            recv_sem=y_recv,
            device_id=(part, z, pr),
            device_id_type=MESH,
        )

    outer_normed = standardize(stack.astype(F32)).astype(BF16)
    factors = dot(outer_normed, operand)
    diagonal = iota((L, L), 0) == iota((L, L), 1)
    valid_column = jnp.concatenate(
        [
            jnp.sum(jnp.where(diagonal, usable_rows[s], 0.0), axis=1, keepdims=True)
            for s in range(S)
        ],
        axis=0,
    )
    residue = iota((T, 128), 0) % I
    tile_lane = iota((T, 128), 1)
    left_mask = jnp.where(tile_lane // PH == residue, valid_column, 0.0)
    JL = 128 // Q
    stacked = []
    for g in range(G):
        left = factors[:, g * 128 : (g + 1) * 128] * left_mask
        right = factors[:, G * 128 : (G + 1) * 128] * jnp.where(
            tile_lane // Q + g * JL == residue, valid_column, 0.0
        )
        stacked.append(jnp.concatenate([left, right], axis=1).astype(BF16))
    stacked = jnp.concatenate(stacked, axis=0)
    out_row = iota((R * 16, G * T), 0)
    in_row = iota((R * 16, G * T), 1)
    in_code = (in_row % L) // I * 16 + (in_row // T) * S + (in_row % T) // L
    message = dot(indicator(out_row == in_code), stacked).astype(BF16)
    message = message.reshape(R, 16, 256)
    lbuf[...] = message[:, :, 0:128]
    rbuf[...] = message[:, :, 128:256]

    def g_copies(k):
        pr, pz = peer(k)
        both = []
        for source, first in ((lbuf.at[pr], 0), (rbuf.at[pz * C // I], 128)):
            both.append(
                pltpu.make_async_remote_copy(
                    src_ref=source,
                    dst_ref=gbuf.at[me, :, pl.ds(first, 128)],
                    send_sem=g_send,
                    recv_sem=g_recv,
                    device_id=(part, pz, pr),
                    device_id_type=MESH,
                )
            )
        return both

    def send_factors(k, carry):
        for copy in g_copies(k):
            copy.start()
        return carry

    lax.fori_loop(1, D, send_factors, 0)
    own_out = pltpu.make_async_copy(ybuf.at[r], y_hbm.at[pl.ds(r * S, S)], local_sem.at[0])
    own_out.start()
    for k in range(1, R):
        y_copy(k).start()
    block_of_columns = z * C // I
    gbuf[me, :, 0:128] = lbuf[r]
    gbuf[me, :, 128:256] = rbuf[block_of_columns]

    rows_i = jnp.concatenate([notes[r * Z + zz, :, 128:256] for zz in range(Z)], axis=0)
    rows_j = jnp.concatenate(
        [notes[block_of_columns * Z + zz, :, 128:256] for zz in range(Z)], axis=0
    )
    counts = dot(rows_i, rows_j, ((0,), (0,)))[:I]
    first_column = lax.rem(z * C, I)
    pick = iota((C, 128), 1) == iota((C, 128), 0) + first_column
    counts = jnp.sum(jnp.where(pick[None], counts[:, None, :], 0.0), axis=-1, keepdims=True)
    inverse = 1.0 / jnp.maximum(counts, 1.0)

    SD = 16 * S
    srow = iota((G * SD, 256), 0)
    code = (srow // S) % 16 * 16 + (srow // SD) * S + srow % S
    regroup = indicator(code == iota((G * SD, 256), 1))
    NJ = C // JL
    loads[3].wait()
    all_but_one(gbuf, g_recv).wait()
    outer = [0.0] * G
    for chunk in range(D // 16):
        rows = gbuf[chunk * 16 : (chunk + 1) * 16].reshape(256, 256)
        ordered = dot(regroup, rows)
        if C == I:
            right = [ordered[t * SD : (t + 1) * SD, 128:256] for t in range(NJ)]
        else:
            grouped[...] = ordered
            first = pl.multiple_of(first_column // JL * SD, 8)
            right = [grouped[pl.ds(first + t * SD, SD), 128:256] for t in range(NJ)]
        right = jnp.concatenate(right, axis=1).astype(BF16)
        for g in range(G):
            left = ordered[g * SD : (g + 1) * SD, 0:128].astype(BF16)
            outer[g] = outer[g] + dot(left, right, ((0,), (0,)))
    low_half = iota((1, 128), 1) < 64
    even = (iota((1, 128), 1) // 32) % 2 == 0
    for t in range(NJ):
        tiles = [outer[g][:, t * 128 : (t + 1) * 128] for g in range(G)]
        for g in (0, 1):
            a, b = tiles[g], tiles[g + 2]
            tiles[g] = jnp.where(low_half, a, pltpu.roll(b, 64, 1))
            tiles[g + 2] = jnp.where(low_half, pltpu.roll(a, 64, 1), b)
        for g in (0, 2):
            a, b = tiles[g], tiles[g + 1]
            tiles[g] = jnp.where(even, a, pltpu.roll(b, 32, 1))
            tiles[g + 1] = jnp.where(even, pltpu.roll(a, 96, 1), b)
        for g in range(JL):
            for i in range(I):
                unfolded[pl.ds((i * C + t * JL + g) * PH, PH), :] = tiles[g][i * PH : (i + 1) * PH]
    couples = jnp.concatenate(
        [unfolded[pl.ds(p, I * C, stride=PH), :] for p in range(PH)], axis=1
    )
    high = couples.astype(BF16)
    low = (couples - high.astype(F32)).astype(BF16)
    update = dot(high, product[...]) + dot(low, product[...])
    pair = edge_ref[...].astype(F32) + update.reshape(I, C, E) * inverse
    pair_ref[...] = pair.astype(BF16)

    own_out.wait()
    all_but_one(ybuf, y_recv).wait()
    all_but_one(xall, x_send).wait()
    all_but_one(ybuf, y_send).wait()
    all_but_one(notes, n_send).wait()
    all_but_one(gbuf, g_send).wait()


def shards(x, edge, homolog, amino, stretch, qkvg, logit, blend, operand, product):
    Z, R = lax.axis_size("seq"), lax.axis_size("res")
    N, I, W = x.shape
    C, E = edge.shape[1:]
    H = logit.shape[1]
    S, L, D = N // R, R * I, R * Z
    vmem = pl.BlockSpec(memory_space=pltpu.VMEM)
    hbm = pl.BlockSpec(memory_space=pl.ANY)
    dma = pltpu.SemaphoreType.DMA
    return pl.pallas_call(
        functools.partial(kernel, Z, R),
        out_shape=(
            jax.ShapeDtypeStruct(x.shape, BF16),
            jax.ShapeDtypeStruct(edge.shape, BF16),
        ),
        in_specs=[hbm, vmem, vmem, vmem, vmem, hbm, vmem, hbm, vmem, hbm],
        out_specs=(hbm, vmem),
        scratch_shapes=[
            pltpu.VMEM((R, S, I, W), BF16),
            pltpu.VMEM(qkvg.shape, BF16),
            pltpu.VMEM(blend.shape, BF16),
            pltpu.VMEM(product.shape, BF16),
            pltpu.VMEM((D, 16, 256), BF16),
            pltpu.VMEM((N, L), F32),
            pltpu.VMEM((H, L, L), F32),
            pltpu.VMEM((R, S, I, W), BF16),
            pltpu.VMEM((R, 16, 128), BF16),
            pltpu.VMEM((R, 16, 128), BF16),
            pltpu.VMEM((D, 16, 256), BF16),
            pltpu.VMEM((4 * 16 * S, 256), F32),
            pltpu.VMEM((I * C * 8, 128), F32),
            dma((4,)),
            dma,
            dma,
            dma,
            dma,
            dma,
            dma,
            dma,
            dma,
        ],
        compiler_params=pltpu.CompilerParams(
            collective_id=0, has_side_effects=True, vmem_limit_bytes=48 * 1024 * 1024
        ),
        cost_estimate=pl.CostEstimate(
            flops=400_000_000, bytes_accessed=1_500_000, transcendentals=200_000
        ),
    )(x, edge, homolog, amino, stretch, qkvg, logit, blend, operand, product)


def solution(mesh):
    in_specs = (
        P(("parts", "seq"), "res", None),
        P(("parts", "res"), "seq", None),
        P(("parts", "seq"), "res"),
        P(("parts", "res")),
        P(),
        P(),
        P(),
        P(),
        P(),
        P(),
    )
    out_specs = (P(("parts", "seq"), "res", None), P(("parts", "res"), "seq", None))
    return jax.shard_map(shards, mesh=mesh, in_specs=in_specs, out_specs=out_specs, check_vma=False)
```

```python
import functools
import math

import jax
import jax.numpy as jnp
from jax import lax
from jax.experimental import pallas as pl
from jax.experimental.pallas import tpu as pltpu
from jax.sharding import PartitionSpec as P

MESH = pl.DeviceIdType.MESH
F32 = jnp.float32
BF16 = jnp.bfloat16


def iota(shape, dim):
    return lax.broadcasted_iota(jnp.int32, shape, dim)


def standardize(values):
    center = jnp.mean(values, axis=-1, keepdims=True)
    shifted = values - center
    spread = jnp.mean(shifted * shifted, axis=-1, keepdims=True)
    return shifted * lax.rsqrt(spread + 1e-05)


def dot(a, b, dims=((1,), (0,)), precision=None):
    return lax.dot_general(a, b, (dims, ((), ())), precision=precision, preferred_element_type=F32)


def indicator(condition):
    return jnp.where(condition, 1.0, 0.0).astype(BF16)


def kernel(
    Z,
    R,
    x_hbm,
    edge_hbm,
    homolog_hbm,
    amino_hbm,
    stretch_hbm,
    qkvg_hbm,
    logit_hbm,
    blend_hbm,
    operand_hbm,
    product_hbm,
    y_hbm,
    pair_ref,
    xall,
    edge_ref,
    homolog_ref,
    amino_ref,
    stretch_ref,
    logit_ref,
    operand_ref,
    qkvg,
    blend,
    product,
    notes,
    usable,
    bias,
    ybuf,
    lbuf,
    rbuf,
    gbuf,
    grouped,
    unfolded,
    local_sem,
    x_send,
    x_recv,
    n_send,
    n_recv,
    y_send,
    y_recv,
    g_send,
    g_recv,
):
    N, I, W = x_hbm.shape
    C, E = edge_hbm.shape[1:]
    H = logit_hbm.shape[0]
    DH = blend_hbm.shape[0] // H
    Q = operand_hbm.shape[0] // 2
    S = N // R
    L = R * I
    D = R * Z
    T = S * L
    G = 128 // Q
    PH = Q // G
    GB = max(1, I * C // 128)
    IG = I // GB

    part = lax.axis_index("parts")
    z = lax.axis_index("seq")
    r = lax.axis_index("res")
    me = r * Z + z

    def peer(k):
        other = lax.rem(me + k, D)
        return other // Z, lax.rem(other, Z)

    barrier = pltpu.get_barrier_semaphore()

    def greet(k, carry):
        pr, pz = peer(k)
        pl.semaphore_signal(barrier, inc=1, device_id=(part, pz, pr), device_id_type=MESH)
        return carry

    lax.fori_loop(1, D, greet, 0)

    loads = [
        pltpu.make_async_copy(x_hbm.at[pl.ds(r * S, S)], xall.at[r], local_sem.at[0]),
        pltpu.make_async_copy(qkvg_hbm, qkvg, local_sem.at[1]),
        pltpu.make_async_copy(blend_hbm, blend, local_sem.at[2]),
        pltpu.make_async_copy(product_hbm, product, local_sem.at[3]),
        pltpu.make_async_copy(edge_hbm, edge_ref, local_sem.at[4]),
        pltpu.make_async_copy(logit_hbm, logit_ref, local_sem.at[5]),
        pltpu.make_async_copy(homolog_hbm, homolog_ref, local_sem.at[6]),
        pltpu.make_async_copy(amino_hbm, amino_ref, local_sem.at[7]),
        pltpu.make_async_copy(operand_hbm, operand_ref, local_sem.at[8]),
        pltpu.make_async_copy(stretch_hbm, stretch_ref, local_sem.at[9]),
    ]
    for load in loads[4:] + loads[:4]:
        load.start()

    for load in loads[4:8]:
        load.wait()
    edge = edge_ref[...].astype(F32).reshape(I * C, E)
    bias_rows = dot(
        logit_ref[...], standardize(edge), ((1,), (1,)), lax.Precision.HIGHEST
    )
    width = IG * C
    pieces = [bias_rows[:, g * width : (g + 1) * width] for g in range(GB)]
    bias_rows = jnp.concatenate(pieces, axis=0) if GB > 1 else pieces[0]
    bias_rows = jnp.pad(bias_rows, ((0, 16 - GB * H), (0, 128 - width)))
    valid = (homolog_ref[...] * amino_ref[...][None, :]).astype(F32)
    notes[me, :, 0:128] = bias_rows.astype(BF16)
    notes[me, :, 128:256] = jnp.pad(valid, ((0, 0), (0, 128 - I))).astype(BF16)

    lane = iota((2 * Q, 128), 1)
    channel = iota((2 * Q, 128), 0)
    spread_left = [indicator(channel == lax.rem(lane, PH) * G + g) for g in range(G)]
    spread_right = indicator(channel == Q + lax.rem(lane, Q))
    spread = jnp.concatenate(spread_left + [spread_right], axis=1)
    loads[8].wait()
    operand = dot(operand_ref[...], spread, ((0,), (0,))).astype(BF16)

    pl.semaphore_wait(barrier, D - 1)

    def x_copy(k):
        pr = lax.rem(r + k, R)
        return pltpu.make_async_remote_copy(
            src_ref=x_hbm.at[pl.ds(pr * S, S)],
            dst_ref=xall.at[r],
            send_sem=x_send,
            recv_sem=x_recv,
            device_id=(part, z, pr),
            device_id_type=MESH,
        )

    def send_notes(k, carry):
        pr, pz = peer(k)
        pltpu.make_async_remote_copy(
            src_ref=notes.at[me],
            dst_ref=notes.at[me],
            send_sem=n_send,
            recv_sem=n_recv,
            device_id=(part, pz, pr),
            device_id_type=MESH,
        ).start()
        return carry

    lax.fori_loop(1, D, send_notes, 0)
    for k in range(1, R):
        x_copy(k).start()

    def all_but_one(ref, sem):
        window = ref.at[pl.ds(0, ref.shape[0] - 1)]
        return pltpu.make_async_copy(window, window, sem)

    loads[0].wait()
    loads[1].wait()
    loads[9].wait()
    all_but_one(xall, x_recv).wait()
    x = jnp.concatenate(
        [xall[rr, s] for s in range(S) for rr in range(R)], axis=0
    ).astype(F32)
    normed = (standardize(x) * stretch_ref[...][None, :]).astype(BF16)
    HW = H * DH
    queries = (dot(normed, qkvg[:, 0:HW]) * (1.0 / math.sqrt(DH))).astype(BF16)
    keys = dot(normed, qkvg[:, HW : 2 * HW]).astype(BF16)
    values = dot(normed, qkvg[:, 2 * HW : 3 * HW]).astype(BF16)
    gating = jax.nn.sigmoid(dot(normed, qkvg[:, 3 * HW : 4 * HW]))

    head_of_lane = iota((1, HW), 1) // DH
    head_masks = [indicator(head_of_lane == h) for h in range(H)]

    def raw_scores(s):
        q = queries[s * L : (s + 1) * L]
        expanded = jnp.concatenate([q * head_masks[h] for h in range(H)], axis=0)
        return dot(expanded, keys[s * L : (s + 1) * L], ((1,), (1,)))

    raw = [raw_scores(s) for s in range(S)]

    all_but_one(notes, n_recv).wait()
    KZ = Z * 128
    row = iota((KZ, L), 0)
    fold = indicator(
        ((row % 128) % C + (row // 128) * C == iota((KZ, L), 1)) & (row % 128 < width)
    )
    own_lane = jnp.where((iota((IG, KZ), 1) % 128) // C == iota((IG, KZ), 0), 1.0, 0.0)
    for rr in range(R):
        wide = jnp.concatenate(
            [notes[rr * Z + zz, :, 0:128] for zz in range(Z)], axis=1
        ).astype(F32)[: GB * H]
        wide = (wide[:, None, :] * own_lane[None]).reshape(GB * H * IG, KZ).astype(BF16)
        block = dot(wide, fold).reshape(GB, H, IG, L)
        for g in range(GB):
            bias[:, pl.ds(rr * I + g * IG, IG), :] = block[g]

    mask_rows = jnp.concatenate([notes[rr * Z + z, :, 128:256] for rr in range(R)], axis=1)
    prow = iota((R * 128, L), 0)
    place = indicator(
        (prow % 128 + (prow // 128) * I == iota((R * 128, L), 1)) & (prow % 128 < I)
    )
    usable[...] = dot(mask_rows, place)
    usable_rows = [usable[pl.ds(r * S + s, 1), :] for s in range(S)]
    pair_bias = bias[...].reshape(H * L, L)

    attended = []
    for s in range(S):
        scores = raw[s] + pair_bias
        scores = jnp.where(usable_rows[s] > 0, scores, -1000000000.0)
        raised = jnp.exp(scores - jnp.max(scores, axis=-1, keepdims=True))
        weights = (raised * (1.0 / jnp.sum(raised, axis=-1, keepdims=True))).astype(BF16)
        mixed = dot(weights, values[s * L : (s + 1) * L])
        total = mixed[0:L] * head_masks[0].astype(F32)
        for h in range(1, H):
            total = total + mixed[h * L : (h + 1) * L] * head_masks[h].astype(F32)
        attended.append(total.astype(BF16))
    attended = jnp.concatenate(attended, axis=0).astype(F32)
    gated = (gating * attended).astype(BF16)
    loads[2].wait()
    stack = (x + dot(gated, blend[...])).astype(BF16)
    for s in range(S):
        for rr in range(R):
            start = s * L + rr * I
            ybuf[rr, s] = stack[start : start + I]

    def y_copy(k):
        pr = lax.rem(r + k, R)
        return pltpu.make_async_remote_copy(
            src_ref=ybuf.at[pr],
            dst_ref=y_hbm.at[pl.ds(r * S, S)],
            send_sem=y_send,
            recv_sem=y_recv,
            device_id=(part, z, pr),
            device_id_type=MESH,
        )

    outer_normed = standardize(stack.astype(F32)).astype(BF16)
    factors = dot(outer_normed, operand)
    diagonal = iota((L, L), 0) == iota((L, L), 1)
    valid_column = jnp.concatenate(
        [
            jnp.sum(jnp.where(diagonal, usable_rows[s], 0.0), axis=1, keepdims=True)
            for s in range(S)
        ],
        axis=0,
    )
    residue = iota((T, 128), 0) % I
    tile_lane = iota((T, 128), 1)
    left_mask = jnp.where(tile_lane // PH == residue, valid_column, 0.0)
    JL = 128 // Q
    stacked = []
    for g in range(G):
        left = factors[:, g * 128 : (g + 1) * 128] * left_mask
        right = factors[:, G * 128 : (G + 1) * 128] * jnp.where(
            tile_lane // Q + g * JL == residue, valid_column, 0.0
        )
        stacked.append(jnp.concatenate([left, right], axis=1).astype(BF16))
    stacked = jnp.concatenate(stacked, axis=0)
    out_row = iota((R * 16, G * T), 0)
    in_row = iota((R * 16, G * T), 1)
    in_code = (in_row % L) // I * 16 + (in_row // T) * S + (in_row % T) // L
    message = dot(indicator(out_row == in_code), stacked).astype(BF16)
    message = message.reshape(R, 16, 256)
    lbuf[...] = message[:, :, 0:128]
    rbuf[...] = message[:, :, 128:256]

    def g_copies(k):
        pr, pz = peer(k)
        both = []
        for source, first in ((lbuf.at[pr], 0), (rbuf.at[pz * C // I], 128)):
            both.append(
                pltpu.make_async_remote_copy(
                    src_ref=source,
                    dst_ref=gbuf.at[me, :, pl.ds(first, 128)],
                    send_sem=g_send,
                    recv_sem=g_recv,
                    device_id=(part, pz, pr),
                    device_id_type=MESH,
                )
            )
        return both

    def send_factors(k, carry):
        for copy in g_copies(k):
            copy.start()
        return carry

    lax.fori_loop(1, D, send_factors, 0)
    own_out = pltpu.make_async_copy(ybuf.at[r], y_hbm.at[pl.ds(r * S, S)], local_sem.at[0])
    own_out.start()
    for k in range(1, R):
        y_copy(k).start()
    block_of_columns = z * C // I
    gbuf[me, :, 0:128] = lbuf[r]
    gbuf[me, :, 128:256] = rbuf[block_of_columns]

    rows_i = jnp.concatenate([notes[r * Z + zz, :, 128:256] for zz in range(Z)], axis=0)
    rows_j = jnp.concatenate(
        [notes[block_of_columns * Z + zz, :, 128:256] for zz in range(Z)], axis=0
    )
    counts = dot(rows_i, rows_j, ((0,), (0,)))[:I]
    first_column = lax.rem(z * C, I)
    pick = iota((C, 128), 1) == iota((C, 128), 0) + first_column
    counts = jnp.sum(jnp.where(pick[None], counts[:, None, :], 0.0), axis=-1, keepdims=True)
    inverse = 1.0 / jnp.maximum(counts, 1.0)

    SD = 16 * S
    srow = iota((G * SD, 256), 0)
    code = (srow // S) % 16 * 16 + (srow // SD) * S + srow % S
    regroup = indicator(code == iota((G * SD, 256), 1))
    NJ = C // JL
    loads[3].wait()
    all_but_one(gbuf, g_recv).wait()
    outer = [0.0] * G
    for chunk in range(D // 16):
        rows = gbuf[chunk * 16 : (chunk + 1) * 16].reshape(256, 256)
        ordered = dot(regroup, rows)
        if C == I:
            right = [ordered[t * SD : (t + 1) * SD, 128:256] for t in range(NJ)]
        else:
            grouped[...] = ordered
            first = pl.multiple_of(first_column // JL * SD, 8)
            right = [grouped[pl.ds(first + t * SD, SD), 128:256] for t in range(NJ)]
        right = jnp.concatenate(right, axis=1).astype(BF16)
        for g in range(G):
            left = ordered[g * SD : (g + 1) * SD, 0:128].astype(BF16)
            outer[g] = outer[g] + dot(left, right, ((0,), (0,)))
    low_half = iota((1, 128), 1) < 64
    even = (iota((1, 128), 1) // 32) % 2 == 0
    for t in range(NJ):
        tiles = [outer[g][:, t * 128 : (t + 1) * 128] for g in range(G)]
        for g in (0, 1):
            a, b = tiles[g], tiles[g + 2]
            tiles[g] = jnp.where(low_half, a, pltpu.roll(b, 64, 1))
            tiles[g + 2] = jnp.where(low_half, pltpu.roll(a, 64, 1), b)
        for g in (0, 2):
            a, b = tiles[g], tiles[g + 1]
            tiles[g] = jnp.where(even, a, pltpu.roll(b, 32, 1))
            tiles[g + 1] = jnp.where(even, pltpu.roll(a, 96, 1), b)
        for g in range(JL):
            for i in range(I):
                unfolded[pl.ds((i * C + t * JL + g) * PH, PH), :] = tiles[g][i * PH : (i + 1) * PH]
    couples = jnp.concatenate(
        [unfolded[pl.ds(p, I * C, stride=PH), :] for p in range(PH)], axis=1
    )
    high = couples.astype(BF16)
    low = (couples - high.astype(F32)).astype(BF16)
    update = dot(high, product[...]) + dot(low, product[...])
    pair = edge_ref[...].astype(F32) + update.reshape(I, C, E) * inverse
    pair_ref[...] = pair.astype(BF16)

    own_out.wait()
    all_but_one(ybuf, y_recv).wait()
    all_but_one(xall, x_send).wait()
    all_but_one(ybuf, y_send).wait()
    all_but_one(notes, n_send).wait()
    all_but_one(gbuf, g_send).wait()


def shards(x, edge, homolog, amino, stretch, qkvg, logit, blend, operand, product):
    logit, operand = logit.T, operand.T
    Z, R = lax.axis_size("seq"), lax.axis_size("res")
    N, I, W = x.shape
    C, E = edge.shape[1:]
    H = logit.shape[0]
    S, L, D = N // R, R * I, R * Z
    vmem = pl.BlockSpec(memory_space=pltpu.VMEM)
    hbm = pl.BlockSpec(memory_space=pltpu.HBM)
    dma = pltpu.SemaphoreType.DMA
    return pl.pallas_call(
        functools.partial(kernel, Z, R),
        out_shape=(
            jax.ShapeDtypeStruct(x.shape, BF16),
            jax.ShapeDtypeStruct(edge.shape, BF16),
        ),
        in_specs=[hbm] * 10,
        out_specs=(hbm, vmem),
        scratch_shapes=[
            pltpu.VMEM((R, S, I, W), BF16),
            pltpu.VMEM(edge.shape, BF16),
            pltpu.VMEM(homolog.shape, jnp.int32),
            pltpu.VMEM(amino.shape, jnp.int32),
            pltpu.VMEM(stretch.shape, F32),
            pltpu.VMEM(logit.shape, F32),
            pltpu.VMEM(operand.shape, BF16),
            pltpu.VMEM(qkvg.shape, BF16),
            pltpu.VMEM(blend.shape, BF16),
            pltpu.VMEM(product.shape, BF16),
            pltpu.VMEM((D, 16, 256), BF16),
            pltpu.VMEM((N, L), F32),
            pltpu.VMEM((H, L, L), F32),
            pltpu.VMEM((R, S, I, W), BF16),
            pltpu.VMEM((R, 16, 128), BF16),
            pltpu.VMEM((R, 16, 128), BF16),
            pltpu.VMEM((D, 16, 256), BF16),
            pltpu.VMEM((4 * 16 * S, 256), F32),
            pltpu.VMEM((I * C * 8, 128), F32),
            dma((10,)),
            dma,
            dma,
            dma,
            dma,
            dma,
            dma,
            dma,
            dma,
        ],
        compiler_params=pltpu.CompilerParams(
            collective_id=0, has_side_effects=True, vmem_limit_bytes=64 * 1024 * 1024
        ),
        cost_estimate=pl.CostEstimate(
            flops=400_000_000, bytes_accessed=1_500_000, transcendentals=200_000
        ),
    )(x, edge, homolog, amino, stretch, qkvg, logit, blend, operand, product)


def solution(mesh):
    in_specs = (
        P(("parts", "seq"), "res", None),
        P(("parts", "res"), "seq", None),
        P(("parts", "seq"), "res"),
        P(("parts", "res")),
        P(),
        P(),
        P(),
        P(),
        P(),
        P(),
    )
    out_specs = (P(("parts", "seq"), "res", None), P(("parts", "res"), "seq", None))
    return jax.shard_map(shards, mesh=mesh, in_specs=in_specs, out_specs=out_specs, check_vma=False)
```

```python
import functools
import math

import jax
import jax.numpy as jnp
from jax import lax
from jax.experimental import pallas as pl
from jax.experimental.pallas import tpu as pltpu
from jax.sharding import PartitionSpec as P

MESH = pl.DeviceIdType.MESH
F32 = jnp.float32
BF16 = jnp.bfloat16


def iota(shape, dim):
    return lax.broadcasted_iota(jnp.int32, shape, dim)


def standardize(values):
    center = jnp.mean(values, axis=-1, keepdims=True)
    shifted = values - center
    spread = jnp.mean(shifted * shifted, axis=-1, keepdims=True)
    return shifted * lax.rsqrt(spread + 1e-05)


def dot(a, b, dims=((1,), (0,)), precision=None):
    return lax.dot_general(a, b, (dims, ((), ())), precision=precision, preferred_element_type=F32)


def indicator(condition):
    return jnp.where(condition, 1.0, 0.0).astype(BF16)


def kernel(
    Z,
    R,
    x_hbm,
    edge_hbm,
    homolog_hbm,
    amino_hbm,
    stretch_hbm,
    qkvg_hbm,
    logit_hbm,
    blend_hbm,
    operand_hbm,
    product_hbm,
    y_hbm,
    pair_ref,
    xall,
    edge_ref,
    homolog_ref,
    amino_ref,
    stretch_ref,
    logit_ref,
    operand_ref,
    qkvg,
    blend,
    product,
    notes,
    usable,
    bias,
    ybuf,
    lbuf,
    rbuf,
    gbuf,
    grouped,
    unfolded,
    local_sem,
    x_send,
    x_recv,
    n_send,
    n_recv,
    y_send,
    y_recv,
    g_send,
    g_recv,
):
    N, I, W = x_hbm.shape
    C, E = edge_hbm.shape[1:]
    H = logit_hbm.shape[0]
    DH = blend_hbm.shape[0] // H
    Q = operand_hbm.shape[0] // 2
    S = N // R
    L = R * I
    D = R * Z
    T = S * L
    G = 128 // Q
    PH = Q // G
    GB = max(1, I * C // 128)
    IG = I // GB

    part = lax.axis_index("parts")
    z = lax.axis_index("seq")
    r = lax.axis_index("res")
    me = r * Z + z

    def peer(k):
        other = lax.rem(me + k, D)
        return other // Z, lax.rem(other, Z)

    barrier = pltpu.get_barrier_semaphore()

    def greet(k, carry):
        pr, pz = peer(k)
        pl.semaphore_signal(barrier, inc=1, device_id=(part, pz, pr), device_id_type=MESH)
        return carry

    lax.fori_loop(1, D, greet, 0)

    loads = [
        pltpu.make_async_copy(x_hbm.at[pl.ds(r * S, S)], xall.at[r], local_sem.at[0]),
        pltpu.make_async_copy(qkvg_hbm, qkvg, local_sem.at[1]),
        pltpu.make_async_copy(blend_hbm, blend, local_sem.at[2]),
        pltpu.make_async_copy(product_hbm, product, local_sem.at[3]),
        pltpu.make_async_copy(edge_hbm, edge_ref, local_sem.at[4]),
        pltpu.make_async_copy(logit_hbm, logit_ref, local_sem.at[5]),
        pltpu.make_async_copy(homolog_hbm, homolog_ref, local_sem.at[6]),
        pltpu.make_async_copy(amino_hbm, amino_ref, local_sem.at[7]),
        pltpu.make_async_copy(operand_hbm, operand_ref, local_sem.at[8]),
        pltpu.make_async_copy(stretch_hbm, stretch_ref, local_sem.at[9]),
    ]
    for load in loads[4:] + loads[:4]:
        load.start()

    for load in loads[4:8]:
        load.wait()
    edge = edge_ref[...].astype(F32).reshape(I * C, E)
    bias_rows = dot(
        logit_ref[...], standardize(edge), ((1,), (1,)), lax.Precision.HIGHEST
    )
    width = IG * C
    pieces = [bias_rows[:, g * width : (g + 1) * width] for g in range(GB)]
    bias_rows = jnp.concatenate(pieces, axis=0) if GB > 1 else pieces[0]
    bias_rows = jnp.pad(bias_rows, ((0, 16 - GB * H), (0, 128 - width)))
    valid = (homolog_ref[...] * amino_ref[...][None, :]).astype(F32)
    notes[me, :, 0:128] = bias_rows.astype(BF16)
    notes[me, :, 128:256] = jnp.pad(valid, ((0, 0), (0, 128 - I))).astype(BF16)

    lane = iota((2 * Q, 128), 1)
    channel = iota((2 * Q, 128), 0)
    spread_left = [indicator(channel == lax.rem(lane, PH) * G + g) for g in range(G)]
    spread_right = indicator(channel == Q + lax.rem(lane, Q))
    spread = jnp.concatenate(spread_left + [spread_right], axis=1)
    loads[8].wait()
    operand = dot(operand_ref[...], spread, ((0,), (0,))).astype(BF16)

    pl.semaphore_wait(barrier, D - 1)

    def x_copy(k):
        pr = lax.rem(r + k, R)
        return pltpu.make_async_remote_copy(
            src_ref=x_hbm.at[pl.ds(pr * S, S)],
            dst_ref=xall.at[r],
            send_sem=x_send,
            recv_sem=x_recv,
            device_id=(part, z, pr),
            device_id_type=MESH,
        )

    def send_notes(k, carry):
        pr, pz = peer(k)
        pltpu.make_async_remote_copy(
            src_ref=notes.at[me],
            dst_ref=notes.at[me],
            send_sem=n_send,
            recv_sem=n_recv,
            device_id=(part, pz, pr),
            device_id_type=MESH,
        ).start()
        return carry

    lax.fori_loop(1, D, send_notes, 0)
    for k in range(1, R):
        x_copy(k).start()

    def all_but_one(ref, sem):
        window = ref.at[pl.ds(0, ref.shape[0] - 1)]
        return pltpu.make_async_copy(window, window, sem)

    loads[0].wait()
    loads[1].wait()
    loads[9].wait()
    all_but_one(xall, x_recv).wait()
    x = jnp.concatenate(
        [xall[rr, s] for s in range(S) for rr in range(R)], axis=0
    ).astype(F32)
    normed = (standardize(x) * stretch_ref[...][None, :]).astype(BF16)
    HW = H * DH
    queries = (dot(normed, qkvg[:, 0:HW]) * (1.0 / math.sqrt(DH))).astype(BF16)
    keys = dot(normed, qkvg[:, HW : 2 * HW]).astype(BF16)
    values = dot(normed, qkvg[:, 2 * HW : 3 * HW]).astype(BF16)
    gating = jax.nn.sigmoid(dot(normed, qkvg[:, 3 * HW : 4 * HW]))

    head_of_lane = iota((1, HW), 1) // DH
    head_masks = [indicator(head_of_lane == h) for h in range(H)]

    def raw_scores(s):
        q = queries[s * L : (s + 1) * L]
        expanded = jnp.concatenate([q * head_masks[h] for h in range(H)], axis=0)
        return dot(expanded, keys[s * L : (s + 1) * L], ((1,), (1,)))

    raw = [raw_scores(s) for s in range(S)]

    all_but_one(notes, n_recv).wait()
    KZ = Z * 128
    row = iota((KZ, L), 0)
    fold = indicator(
        ((row % 128) % C + (row // 128) * C == iota((KZ, L), 1)) & (row % 128 < width)
    )
    own_lane = jnp.where((iota((IG, KZ), 1) % 128) // C == iota((IG, KZ), 0), 1.0, 0.0)
    for rr in range(R):
        wide = jnp.concatenate(
            [notes[rr * Z + zz, :, 0:128] for zz in range(Z)], axis=1
        ).astype(F32)[: GB * H]
        wide = (wide[:, None, :] * own_lane[None]).reshape(GB * H * IG, KZ).astype(BF16)
        block = dot(wide, fold).reshape(GB, H, IG, L)
        for g in range(GB):
            bias[:, pl.ds(rr * I + g * IG, IG), :] = block[g]

    mask_rows = jnp.concatenate([notes[rr * Z + z, :, 128:256] for rr in range(R)], axis=1)
    prow = iota((R * 128, L), 0)
    place = indicator(
        (prow % 128 + (prow // 128) * I == iota((R * 128, L), 1)) & (prow % 128 < I)
    )
    usable[...] = dot(mask_rows, place)
    usable_rows = [usable[pl.ds(r * S + s, 1), :] for s in range(S)]
    pair_bias = bias[...].reshape(H * L, L)

    attended = []
    for s in range(S):
        scores = raw[s] + pair_bias
        scores = jnp.where(usable_rows[s] > 0, scores, -1000000000.0)
        raised = jnp.exp(scores - jnp.max(scores, axis=-1, keepdims=True))
        weights = (raised * (1.0 / jnp.sum(raised, axis=-1, keepdims=True))).astype(BF16)
        mixed = dot(weights, values[s * L : (s + 1) * L])
        total = mixed[0:L] * head_masks[0].astype(F32)
        for h in range(1, H):
            total = total + mixed[h * L : (h + 1) * L] * head_masks[h].astype(F32)
        attended.append(total.astype(BF16))
    attended = jnp.concatenate(attended, axis=0).astype(F32)
    gated = (gating * attended).astype(BF16)
    loads[2].wait()
    stack = (x + dot(gated, blend[...])).astype(BF16)
    for s in range(S):
        for rr in range(R):
            start = s * L + rr * I
            ybuf[rr, s] = stack[start : start + I]

    def y_copy(k):
        pr = lax.rem(r + k, R)
        return pltpu.make_async_remote_copy(
            src_ref=ybuf.at[pr],
            dst_ref=y_hbm.at[pl.ds(r * S, S)],
            send_sem=y_send,
            recv_sem=y_recv,
            device_id=(part, z, pr),
            device_id_type=MESH,
        )

    own_out = pltpu.make_async_copy(ybuf.at[r], y_hbm.at[pl.ds(r * S, S)], local_sem.at[0])
    own_out.start()
    for k in range(1, R):
        y_copy(k).start()

    outer_normed = standardize(stack.astype(F32)).astype(BF16)
    factors = dot(outer_normed, operand)
    diagonal = iota((L, L), 0) == iota((L, L), 1)
    valid_column = jnp.concatenate(
        [
            jnp.sum(jnp.where(diagonal, usable_rows[s], 0.0), axis=1, keepdims=True)
            for s in range(S)
        ],
        axis=0,
    )
    residue = iota((T, 128), 0) % I
    tile_lane = iota((T, 128), 1)
    left_mask = jnp.where(tile_lane // PH == residue, valid_column, 0.0)
    JL = 128 // Q
    stacked = []
    for g in range(G):
        left = factors[:, g * 128 : (g + 1) * 128] * left_mask
        right = factors[:, G * 128 : (G + 1) * 128] * jnp.where(
            tile_lane // Q + g * JL == residue, valid_column, 0.0
        )
        stacked.append(jnp.concatenate([left, right], axis=1).astype(BF16))
    stacked = jnp.concatenate(stacked, axis=0)
    out_row = iota((R * 16, G * T), 0)
    in_row = iota((R * 16, G * T), 1)
    in_code = (in_row % L) // I * 16 + (in_row // T) * S + (in_row % T) // L
    message = dot(indicator(out_row == in_code), stacked).astype(BF16)
    message = message.reshape(R, 16, 256)
    lbuf[...] = message[:, :, 0:128]
    rbuf[...] = message[:, :, 128:256]

    def g_copies(k):
        pr, pz = peer(k)
        both = []
        for source, first in ((lbuf.at[pr], 0), (rbuf.at[pz * C // I], 128)):
            both.append(
                pltpu.make_async_remote_copy(
                    src_ref=source,
                    dst_ref=gbuf.at[me, :, pl.ds(first, 128)],
                    send_sem=g_send,
                    recv_sem=g_recv,
                    device_id=(part, pz, pr),
                    device_id_type=MESH,
                )
            )
        return both

    def send_factors(k, carry):
        for copy in g_copies(k):
            copy.start()
        return carry

    lax.fori_loop(1, D, send_factors, 0)
    block_of_columns = z * C // I
    gbuf[me, :, 0:128] = lbuf[r]
    gbuf[me, :, 128:256] = rbuf[block_of_columns]

    rows_i = jnp.concatenate([notes[r * Z + zz, :, 128:256] for zz in range(Z)], axis=0)
    rows_j = jnp.concatenate(
        [notes[block_of_columns * Z + zz, :, 128:256] for zz in range(Z)], axis=0
    )
    counts = dot(rows_i, rows_j, ((0,), (0,)))[:I]
    first_column = lax.rem(z * C, I)
    pick = iota((C, 128), 1) == iota((C, 128), 0) + first_column
    counts = jnp.sum(jnp.where(pick[None], counts[:, None, :], 0.0), axis=-1, keepdims=True)
    inverse = 1.0 / jnp.maximum(counts, 1.0)

    SD = 16 * S
    srow = iota((G * SD, 256), 0)
    code = (srow // S) % 16 * 16 + (srow // SD) * S + srow % S
    regroup = indicator(code == iota((G * SD, 256), 1))
    NJ = C // JL
    loads[3].wait()
    all_but_one(gbuf, g_recv).wait()
    outer = [0.0] * G
    for chunk in range(D // 16):
        rows = gbuf[chunk * 16 : (chunk + 1) * 16].reshape(256, 256)
        ordered = dot(regroup, rows)
        if C == I:
            right = [ordered[t * SD : (t + 1) * SD, 128:256] for t in range(NJ)]
        else:
            grouped[...] = ordered
            first = pl.multiple_of(first_column // JL * SD, 8)
            right = [grouped[pl.ds(first + t * SD, SD), 128:256] for t in range(NJ)]
        right = jnp.concatenate(right, axis=1).astype(BF16)
        for g in range(G):
            left = ordered[g * SD : (g + 1) * SD, 0:128].astype(BF16)
            outer[g] = outer[g] + dot(left, right, ((0,), (0,)))
    low_half = iota((1, 128), 1) < 64
    even = (iota((1, 128), 1) // 32) % 2 == 0
    for t in range(NJ):
        tiles = [outer[g][:, t * 128 : (t + 1) * 128] for g in range(G)]
        for g in (0, 1):
            a, b = tiles[g], tiles[g + 2]
            tiles[g] = jnp.where(low_half, a, pltpu.roll(b, 64, 1))
            tiles[g + 2] = jnp.where(low_half, pltpu.roll(a, 64, 1), b)
        for g in (0, 2):
            a, b = tiles[g], tiles[g + 1]
            tiles[g] = jnp.where(even, a, pltpu.roll(b, 32, 1))
            tiles[g + 1] = jnp.where(even, pltpu.roll(a, 96, 1), b)
        for g in range(JL):
            for i in range(I):
                unfolded[pl.ds((i * C + t * JL + g) * PH, PH), :] = tiles[g][i * PH : (i + 1) * PH]
    couples = jnp.concatenate(
        [unfolded[pl.ds(p, I * C, stride=PH), :] for p in range(PH)], axis=1
    )
    high = couples.astype(BF16)
    low = (couples - high.astype(F32)).astype(BF16)
    update = dot(high, product[...]) + dot(low, product[...])
    pair = edge_ref[...].astype(F32) + update.reshape(I, C, E) * inverse
    pair_ref[...] = pair.astype(BF16)

    own_out.wait()
    all_but_one(ybuf, y_recv).wait()
    all_but_one(xall, x_send).wait()
    all_but_one(ybuf, y_send).wait()
    all_but_one(notes, n_send).wait()
    all_but_one(gbuf, g_send).wait()


def shards(x, edge, homolog, amino, stretch, qkvg, logit, blend, operand, product):
    logit, operand = logit.T, operand.T
    Z, R = lax.axis_size("seq"), lax.axis_size("res")
    N, I, W = x.shape
    C, E = edge.shape[1:]
    H = logit.shape[0]
    S, L, D = N // R, R * I, R * Z
    vmem = pl.BlockSpec(memory_space=pltpu.VMEM)
    hbm = pl.BlockSpec(memory_space=pltpu.HBM)
    dma = pltpu.SemaphoreType.DMA
    return pl.pallas_call(
        functools.partial(kernel, Z, R),
        out_shape=(
            jax.ShapeDtypeStruct(x.shape, BF16),
            jax.ShapeDtypeStruct(edge.shape, BF16),
        ),
        in_specs=[hbm] * 10,
        out_specs=(hbm, vmem),
        scratch_shapes=[
            pltpu.VMEM((R, S, I, W), BF16),
            pltpu.VMEM(edge.shape, BF16),
            pltpu.VMEM(homolog.shape, jnp.int32),
            pltpu.VMEM(amino.shape, jnp.int32),
            pltpu.VMEM(stretch.shape, F32),
            pltpu.VMEM(logit.shape, F32),
            pltpu.VMEM(operand.shape, BF16),
            pltpu.VMEM(qkvg.shape, BF16),
            pltpu.VMEM(blend.shape, BF16),
            pltpu.VMEM(product.shape, BF16),
            pltpu.VMEM((D, 16, 256), BF16),
            pltpu.VMEM((N, L), F32),
            pltpu.VMEM((H, L, L), F32),
            pltpu.VMEM((R, S, I, W), BF16),
            pltpu.VMEM((R, 16, 128), BF16),
            pltpu.VMEM((R, 16, 128), BF16),
            pltpu.VMEM((D, 16, 256), BF16),
            pltpu.VMEM((4 * 16 * S, 256), F32),
            pltpu.VMEM((I * C * 8, 128), F32),
            dma((10,)),
            dma,
            dma,
            dma,
            dma,
            dma,
            dma,
            dma,
            dma,
        ],
        compiler_params=pltpu.CompilerParams(
            collective_id=0, has_side_effects=True, vmem_limit_bytes=64 * 1024 * 1024
        ),
        cost_estimate=pl.CostEstimate(
            flops=400_000_000, bytes_accessed=1_500_000, transcendentals=200_000
        ),
    )(x, edge, homolog, amino, stretch, qkvg, logit, blend, operand, product)


def solution(mesh):
    in_specs = (
        P(("parts", "seq"), "res", None),
        P(("parts", "res"), "seq", None),
        P(("parts", "seq"), "res"),
        P(("parts", "res")),
        P(),
        P(),
        P(),
        P(),
        P(),
        P(),
    )
    out_specs = (P(("parts", "seq"), "res", None), P(("parts", "res"), "seq", None))
    return jax.shard_map(shards, mesh=mesh, in_specs=in_specs, out_specs=out_specs, check_vma=False)
```
